128 devices in a mesh: chan: 16 (over x_lo, z, core), seg: 8 (over y, x_hi).
Axes of the slice: x: 4 (x_hi: 2, x_lo: 2; x = x_hi * 2 + x_lo), y: 4, z: 4, core: 2. Of those that a mesh axis runs over, the one named last changes fastest.
Arguments:
- strain_rate: bfloat16 [1536, 270336], P('chan', 'seg'), may hold values from -56 to 56
- window_starts: int32 [512], P('seg'), may hold values from 0 to 128
Outputs:
- cross_spectra: float32 [96, 2, 1536, 1536], P('seg', None, 'chan')
The draws below stay inside these ranges and needn't reach their ends.
All inputs are finite; a program needn't handle non-finite values.
Results may differ from the reference program's by a relative error of at most 0.00096.
Values may be sent and summed in bfloat16 or wider, within the bound.
No kernel may reach another device: no remote copies, remote signals or barrier semaphores. Data moves between devices by JAX's collectives and lax.ppermute only.
A program may use at most 192 MiB of HBM per device.

```python
import math
import jax
import jax.numpy as jnp
from jax import lax

WINS_DEV = 64
WIN = 1024
F = 96
K0 = 10
SEG_LEN = 33792
CHANNELS = 1536
SEGMENTS = 8
WINDOWS = 512
SAMPLES = 270336


def draw_strain_rate(key, part):
    key = jax.random.fold_in(key, 11)
    wave_key, noise_key, scale_key = jax.random.split(key, 3)
    wave_length = SAMPLES + CHANNELS // 2 + 1
    wave = jax.random.truncated_normal(wave_key, -4.0, 4.0, (wave_length,), jnp.float32)
    local_noise = jax.random.truncated_normal(noise_key, -4.0, 4.0, (CHANNELS, SAMPLES), jnp.float32)

    def delayed(channel):
        return lax.dynamic_slice_in_dim(wave, channel // 2, SAMPLES, 0)
    delayed_wave = jax.vmap(delayed)(jnp.arange(CHANNELS, dtype=jnp.int32))
    levels = jnp.exp(jax.random.uniform(scale_key, (SAMPLES // (WIN // 4),), jnp.float32, 0.0, math.log(10.0)))
    envelope = jnp.repeat(levels, WIN // 4)
    return ((0.8 * delayed_wave + 0.6 * local_noise) * envelope[None, :]).astype(jnp.bfloat16)


def plant(array, rng, least, top_value):
    longest = array.shape.index(max(array.shape))
    spots = []
    for shift in (0, 1):
        where = [jax.random.randint(jax.random.fold_in(rng, axis), (), 0, length) for axis, length in enumerate(array.shape)]
        where[longest] = (where[longest] + shift) % array.shape[longest]
        spots.append(tuple(where))
    return array.at[spots[0]].set(least).at[spots[1]].set(top_value)


def setup_inputs(seed: int = 0) -> dict:
    streams_of = jax.random.split(jax.random.key(seed), 3)
    return {
        "strain_rate": draw_strain_rate(jax.random.fold_in(streams_of[2], 71), 0),
        "window_starts": plant(jax.random.randint(streams_of[1], (WINDOWS,), 0, (SEG_LEN - WIN) // (WIN // 4) + 1), jax.random.fold_in(streams_of[1], 1), 0, ((SEG_LEN - WIN) // (WIN // 4) + 1) - 1).astype(jnp.int32),
    }


EPSILON = 1e-06
CLIP_LEVEL = 1.5

def fourier_table(length, first_bin, bin_count):
    sample_ids = jnp.arange(length, dtype=jnp.int32)
    bin_ids = first_bin + jnp.arange(bin_count, dtype=jnp.int32)
    phase_turns = (bin_ids[:, None] * sample_ids[None, :] % length).astype(jnp.float32) * (2.0 * math.pi / length)
    return jnp.concatenate([jnp.cos(phase_turns), -jnp.sin(phase_turns)], 0).astype(jnp.bfloat16)

def whiten_windows(samples, starts, fourier_rows):
    length = fourier_rows.shape[1]
    quarter = length // 4
    blocks = samples.reshape(samples.shape[0], samples.shape[1] // quarter, quarter)
    block_index = starts.astype(jnp.int32)[:, None] + jnp.arange(4, dtype=jnp.int32)[None, :]
    windows = jnp.take(blocks, block_index, axis=1).reshape(samples.shape[0], starts.shape[0], length).astype(jnp.float32)
    spread = jnp.sqrt(lax.optimization_barrier(jnp.mean(windows * windows, -1, keepdims=True)) + EPSILON)
    hann_window = 0.5 - 0.5 * jnp.cos(jnp.arange(length, dtype=jnp.float32) * (2.0 * math.pi / length))
    tapered = (jnp.clip(windows, -CLIP_LEVEL * spread, CLIP_LEVEL * spread) * hann_window).astype(jnp.bfloat16)
    spectrum = lax.dot_general(fourier_rows.astype(jnp.float32), tapered.astype(jnp.float32), (((1,), (2,)), ((), ())), preferred_element_type=jnp.float32)
    band_power = lax.optimization_barrier(jnp.mean(spectrum * spectrum, 0, keepdims=True)) + EPSILON
    return (spectrum / jnp.sqrt(band_power)).astype(jnp.bfloat16)

def reference(strain_rate, window_starts):
    fourier_rows = fourier_table(WIN, K0, F)

    def one_segment(segment):
        first_sample = (segment * SEG_LEN).astype(jnp.int32)
        samples = lax.dynamic_slice_in_dim(strain_rate, first_sample, SEG_LEN, 1)
        first_window = (segment * WINS_DEV).astype(jnp.int32)
        starts = lax.dynamic_slice_in_dim(window_starts, first_window, WINS_DEV, 0)
        return whiten_windows(samples, starts, fourier_rows)
    per_segment = lax.map(one_segment, jnp.arange(SEGMENTS, dtype=jnp.int32))
    spectra = jnp.moveaxis(per_segment, 0, 2).reshape(2 * F, CHANNELS, WINDOWS)

    def one_bin(bin_rows):
        real_rows = bin_rows[0].astype(jnp.float32)
        imag_rows = bin_rows[1].astype(jnp.float32)
        real_part = jnp.dot(real_rows, real_rows.T, preferred_element_type=jnp.float32) + jnp.dot(imag_rows, imag_rows.T, preferred_element_type=jnp.float32)
        imag_part = jnp.dot(imag_rows, real_rows.T, preferred_element_type=jnp.float32) - jnp.dot(real_rows, imag_rows.T, preferred_element_type=jnp.float32)
        return jnp.stack([real_part, imag_part], 0)
    stacked = lax.map(one_bin, (spectra[:F], spectra[F:]))
    return stacked / WINDOWS
```

```python
import functools
import math

import jax
import jax.numpy as jnp
import numpy as np
from jax import lax
from jax.experimental import pallas as pl
from jax.experimental.pallas import tpu as pltpu
from jax.sharding import PartitionSpec as P
import ml_dtypes

WIN = 1024
QUARTER = WIN // 4
F = 96
K0 = 10
EPSILON = 1e-06
CLIP_LEVEL = 1.5
LANES = 128
GROUP = 32


def fourier_columns():
    n = np.arange(WIN, dtype=np.int64)
    k = K0 + np.arange(F, dtype=np.int64)
    m = (n[:, None] * k[None, :]) % WIN
    phase = (m.astype(np.float32) * np.float32(2.0 * math.pi / WIN)).astype(np.float64)
    table = np.zeros((WIN, 2 * LANES), np.float32)
    table[:, :F] = np.cos(phase)
    table[:, LANES : LANES + F] = -np.sin(phase)
    return table.astype(ml_dtypes.bfloat16)


def hann_row():
    phase = (np.arange(WIN, dtype=np.float32) * np.float32(2.0 * math.pi / WIN)).astype(np.float64)
    return (0.5 - 0.5 * np.cos(phase)).astype(np.float32)[None, :]


def spectra_kernel(starts, samples, table, hann, out, taps, real, imag, staged):
    group = samples.shape[0]
    windows = starts.shape[0]

    def one_window(w, _):
        first = pl.multiple_of(starts[w] * QUARTER, QUARTER)
        win = samples[:, pl.ds(first, WIN)].astype(jnp.float32)
        power = jnp.sum(win * win, -1, keepdims=True) * (1.0 / WIN)
        level = CLIP_LEVEL * jnp.sqrt(power + EPSILON)
        tap = jnp.clip(win, -level, level) * hann[...]
        taps[pl.ds(pl.multiple_of(w * group, group), group), :] = tap.astype(jnp.bfloat16)
        return 0

    lax.fori_loop(0, windows, one_window, 0, unroll=2)

    rows = 512

    def one_dot(i, _):
        at = pl.ds(pl.multiple_of(i * rows, rows), rows)
        spec = jnp.dot(taps[at, :], table[...], preferred_element_type=jnp.float32)
        real[at, :] = spec[:, :LANES]
        imag[at, :] = spec[:, LANES:]
        return 0

    lax.fori_loop(0, windows * group // rows, one_dot, 0)

    def one_channel(c, _):
        at = pl.ds(c, windows, stride=group)
        both = jnp.concatenate([real[at, :], imag[at, :]], 0)
        turned = both.T[:F]
        total = jnp.sum(turned * turned, 0, keepdims=True)
        total = total + pltpu.roll(total, windows, 1)
        scale = lax.rsqrt(total * (1.0 / (2 * F)) + EPSILON)
        staged[pl.ds(c, F, stride=group), :] = turned * scale
        return 0

    lax.fori_loop(0, group, one_channel, 0, unroll=2)
    out[...] = staged[...].reshape(F, group, LANES).astype(jnp.bfloat16)


def local_spectra(samples, starts):
    channels, length = samples.shape
    windows = starts.shape[0]
    return pl.pallas_call(
        spectra_kernel,
        grid=(channels // GROUP,),
        in_specs=[
            pl.BlockSpec(memory_space=pltpu.SMEM),
            pl.BlockSpec((GROUP, length), lambda g: (g, 0)),
            pl.BlockSpec((WIN, 2 * LANES), lambda g: (0, 0)),
            pl.BlockSpec((1, WIN), lambda g: (0, 0)),
        ],
        out_specs=pl.BlockSpec((F, GROUP, LANES), lambda g: (0, g, 0)),
        out_shape=jax.ShapeDtypeStruct((F, channels, LANES), jnp.bfloat16),
        scratch_shapes=[
            pltpu.VMEM((windows * GROUP, WIN), jnp.bfloat16),
            pltpu.VMEM((windows * GROUP, LANES), jnp.float32),
            pltpu.VMEM((windows * GROUP, LANES), jnp.float32),
            pltpu.VMEM((F * GROUP, LANES), jnp.float32),
        ],
        compiler_params=pltpu.CompilerParams(vmem_limit_bytes=48 * 1024 * 1024),
        name="spectra",
    )(starts, samples, jnp.asarray(fourier_columns()), jnp.asarray(hann_row()))


def merge_kernel(parts, out):
    out[0] = jnp.concatenate([parts[s, 0] for s in range(parts.shape[0])], 1)


def merged(parts):
    segments, bins, channels, lanes = parts.shape
    return pl.pallas_call(
        merge_kernel,
        grid=(bins,),
        in_specs=[pl.BlockSpec((segments, 1, channels, lanes), lambda b: (0, b, 0, 0))],
        out_specs=pl.BlockSpec((1, channels, segments * lanes), lambda b: (b, 0, 0)),
        out_shape=jax.ShapeDtypeStruct((bins, channels, segments * lanes), parts.dtype),
        name="merge",
    )(parts)


def rotated(own):
    parts = []
    for s in range(own.shape[1] // LANES):
        tile = own[:, s * LANES : (s + 1) * LANES].astype(jnp.float32)
        lane = lax.broadcasted_iota(jnp.int32, tile.shape, 1)
        tile = pltpu.roll(tile, LANES // 2, 1)
        parts.append(jnp.where(lane < LANES // 2, tile, -tile).astype(jnp.bfloat16))
    return jnp.concatenate(parts, 1)


def cross_kernel(scale, own, others, out):
    mine = own[0]
    rows = mine.shape[0]
    left = jnp.concatenate([mine, rotated(mine)], 0)
    right = others[:, 0].reshape(others.shape[0] * rows, mine.shape[1])
    acc = lax.dot_general(left, right, (((1,), (1,)), ((), ())), preferred_element_type=jnp.float32)
    out[0] = (acc * scale).reshape(2, rows, acc.shape[1])


def cross(own, everyone, window_count):
    bins, rows, depth = own.shape
    devices = everyone.shape[0]
    return pl.pallas_call(
        functools.partial(cross_kernel, 1.0 / window_count),
        grid=(bins,),
        in_specs=[
            pl.BlockSpec((1, rows, depth), lambda b: (b, 0, 0)),
            pl.BlockSpec((devices, 1, rows, depth), lambda b: (0, b, 0, 0)),
        ],
        out_specs=pl.BlockSpec((1, 2, rows, devices * rows), lambda b: (b, 0, 0, 0)),
        out_shape=jax.ShapeDtypeStruct((bins, 2, rows, devices * rows), jnp.float32),
        compiler_params=pltpu.CompilerParams(vmem_limit_bytes=48 * 1024 * 1024),
        name="cross",
    )(own, everyone)


def local(strain_rate, window_starts):
    spectra = local_spectra(strain_rate, window_starts)
    segments = lax.axis_size("seg")
    channels = spectra.shape[1]
    parts = lax.all_to_all(spectra, "seg", split_axis=0, concat_axis=0, tiled=True)
    parts = parts.reshape(segments, F // segments, channels, LANES)
    own = merged(parts)
    everyone = lax.all_gather(own, "chan")
    return cross(own, everyone, segments * window_starts.shape[0])


def solution(mesh):
    in_specs = (P("chan", "seg"), P("seg"))
    out_specs = P("seg", None, "chan", None)
    return jax.shard_map(local, mesh=mesh, in_specs=in_specs, out_specs=out_specs, check_vma=False)
```

```python
import functools
import math

import jax
import jax.numpy as jnp
import numpy as np
from jax import lax
from jax.experimental import pallas as pl
from jax.experimental.pallas import tpu as pltpu
from jax.sharding import PartitionSpec as P
import ml_dtypes

WIN = 1024
QUARTER = WIN // 4
F = 96
K0 = 10
EPSILON = 1e-06
CLIP_LEVEL = 1.5
LANES = 128
GROUP = 32
BATCH = 16
STRIDE = 40


def fourier_columns():
    n = np.arange(WIN, dtype=np.int64)
    k = K0 + np.arange(F, dtype=np.int64)
    m = (n[:, None] * k[None, :]) % WIN
    phase = (m.astype(np.float32) * np.float32(2.0 * math.pi / WIN)).astype(np.float64)
    table = np.zeros((WIN, 2 * LANES), np.float32)
    table[:, :F] = np.cos(phase)
    table[:, LANES : LANES + F] = -np.sin(phase)
    return table.astype(ml_dtypes.bfloat16)


def hann_row():
    phase = (np.arange(WIN, dtype=np.float32) * np.float32(2.0 * math.pi / WIN)).astype(np.float64)
    return (0.5 - 0.5 * np.cos(phase)).astype(np.float32)[None, :]


def spectra_kernel(starts, samples, table, hann, out_b, out_a, taps, real, imag, staged):
    group = samples.shape[0]
    windows = starts.shape[0]

    def some_windows(i, _):
        for k in range(BATCH):
            first = pl.multiple_of(starts[i * BATCH + k] * QUARTER, QUARTER)
            win = samples[:, pl.ds(first, WIN)].astype(jnp.float32)
            power = jnp.sum(win * win, -1, keepdims=True) * (1.0 / WIN)
            level = CLIP_LEVEL * jnp.sqrt(power + EPSILON)
            tap = jnp.clip(win, -level, level) * hann[...]
            taps[k * group : (k + 1) * group, :] = tap.astype(jnp.bfloat16)
        spec = jnp.dot(taps[...], table[...], preferred_element_type=jnp.float32)
        for k in range(BATCH):
            at = pl.ds(pl.multiple_of((i * BATCH + k) * STRIDE, 8), group)
            real[at, :] = spec[k * group : (k + 1) * group, :LANES]
            imag[at, :] = spec[k * group : (k + 1) * group, LANES:]
        return 0

    lax.fori_loop(0, windows // BATCH, some_windows, 0)

    def one_channel(c, _):
        at = pl.ds(c, windows, stride=STRIDE)
        both = jnp.concatenate([real[at, :], imag[at, :]], 0)
        turned = both.T[:F]
        total = jnp.sum(turned * turned, 0, keepdims=True)
        total = total + pltpu.roll(total, windows, 1)
        scale = lax.rsqrt(total * (1.0 / (2 * F)) + EPSILON)
        staged[pl.ds(c, F, stride=STRIDE), :] = turned * scale
        return 0

    lax.fori_loop(0, group, one_channel, 0, unroll=16)

    segments, first = out_b.shape[:2]
    bins = F // segments
    for s in range(segments):
        for b in range(bins):
            value = staged[pl.ds((s * bins + b) * STRIDE, group), :].astype(jnp.bfloat16)
            if b < first:
                out_b[s, b] = value
            else:
                out_a[s, b - first] = value


def local_spectra(samples, starts, segments, first):
    channels, length = samples.shape
    windows = starts.shape[0]
    counts = (first, F // segments - first)
    return pl.pallas_call(
        spectra_kernel,
        grid=(channels // GROUP,),
        in_specs=[
            pl.BlockSpec(memory_space=pltpu.SMEM),
            pl.BlockSpec((GROUP, length), lambda g: (g, 0)),
            pl.BlockSpec((WIN, 2 * LANES), lambda g: (0, 0)),
            pl.BlockSpec((1, WIN), lambda g: (0, 0)),
        ],
        out_specs=[
            pl.BlockSpec((segments, n, GROUP, LANES), lambda g: (0, 0, g, 0)) for n in counts
        ],
        out_shape=[
            jax.ShapeDtypeStruct((segments, n, channels, LANES), jnp.bfloat16) for n in counts
        ],
        scratch_shapes=[
            pltpu.VMEM((BATCH * GROUP, WIN), jnp.bfloat16),
            pltpu.VMEM((windows * STRIDE, LANES), jnp.float32),
            pltpu.VMEM((windows * STRIDE, LANES), jnp.float32),
            pltpu.VMEM((F * STRIDE, LANES), jnp.float32),
        ],
        compiler_params=pltpu.CompilerParams(vmem_limit_bytes=48 * 1024 * 1024),
        name="spectra",
    )(starts, samples, jnp.asarray(fourier_columns()), jnp.asarray(hann_row()))


def rotated(own):
    parts = []
    for s in range(own.shape[1] // LANES):
        tile = own[:, s * LANES : (s + 1) * LANES].astype(jnp.float32)
        lane = lax.broadcasted_iota(jnp.int32, tile.shape, 1)
        tile = pltpu.roll(tile, LANES // 2, 1)
        parts.append(jnp.where(lane < LANES // 2, tile, -tile).astype(jnp.bfloat16))
    return jnp.concatenate(parts, 1)


def after_kernel(*refs):
    del refs


def together(*values):
    return pl.pallas_call(
        after_kernel,
        in_specs=[pl.BlockSpec(memory_space=pl.ANY)] * len(values),
        out_specs=[pl.BlockSpec(memory_space=pl.ANY)] * len(values),
        out_shape=[jax.ShapeDtypeStruct(v.shape, v.dtype) for v in values],
        input_output_aliases={i: i for i in range(len(values))},
        name="together",
    )(*values)


def after(value, *first):
    return pl.pallas_call(
        after_kernel,
        in_specs=[pl.BlockSpec(memory_space=pl.ANY)] * (1 + len(first)),
        out_specs=pl.BlockSpec(memory_space=pl.ANY),
        out_shape=jax.ShapeDtypeStruct(value.shape, value.dtype),
        input_output_aliases={0: 0},
        name="after",
    )(value, *first)


def stack(scale, own, right):
    segments, rows = own.shape[0], own.shape[2]
    mine = jnp.concatenate([own[s, 0] for s in range(segments)], 1)
    left = jnp.concatenate([mine, rotated(mine)], 0)
    acc = lax.dot_general(left, right, (((1,), (1,)), ((), ())), preferred_element_type=jnp.float32)
    return (acc * scale).reshape(2, rows, acc.shape[1])


def gathered_kernel(scale, place, own, others, *refs):
    del place
    segments = own.shape[0]
    columns = others.shape[0] * others.shape[3]
    right = [others[:, s, 0].reshape(columns, LANES) for s in range(segments)]
    refs[-1][0] = stack(scale, own, jnp.concatenate(right, 1))


def pieces_kernel(scale, place, own, *refs):
    pieces = refs[:8]
    out, buf, sems = refs[-3:]
    step = pl.program_id(0)
    z, core = place[1], place[2]

    def copies(b, slot):
        made = []
        for c in range(2):
            for i in range(4):
                at = lax.rem(z + i, 4) * 2 + (core if c == 0 else 1 - core)
                made.append(
                    pltpu.make_async_copy(
                        pieces[4 * c + i].at[:, b], buf.at[slot, at], sems.at[slot, 4 * c + i]
                    )
                )
        return made

    slot = lax.rem(step, 2)

    @pl.when(step == 0)
    def _():
        for copy in copies(0, 0):
            copy.start()

    @pl.when(step + 1 < pl.num_programs(0))
    def _():
        for copy in copies(step + 1, 1 - slot):
            copy.start()

    for copy in copies(step, slot):
        copy.wait()

    segments = own.shape[0]
    columns = buf.shape[1] * buf.shape[3]
    right = [buf[slot, :, s].reshape(columns, LANES) for s in range(segments)]
    out[0] = stack(scale, own, jnp.concatenate(right, 1))


def cross(place, own, others, base, first_bin, *, all_bins, chan, window_count):
    segments, bins, rows, lanes = own.shape
    half = chan // 2
    bases = [] if base is None else [base]
    anywhere = pl.BlockSpec(memory_space=pl.ANY)
    if isinstance(others, list):
        kernel = pieces_kernel
        specs = [anywhere] * len(others)
        scratch = [
            pltpu.VMEM((2, half, segments, rows, lanes), own.dtype),
            pltpu.SemaphoreType.DMA((2, len(others))),
        ]
    else:
        kernel = gathered_kernel
        specs = [pl.BlockSpec((half, segments, 1, rows, lanes), lambda b, at: (0, 0, b, 0, 0))]
        others = [others]
        scratch = []
    return pl.pallas_call(
        functools.partial(kernel, 1.0 / window_count),
        grid_spec=pltpu.PrefetchScalarGridSpec(
            num_scalar_prefetch=1,
            grid=(bins,),
            in_specs=[pl.BlockSpec((segments, 1, rows, lanes), lambda b, at: (0, b, 0, 0))]
            + specs
            + [anywhere] * len(bases),
            out_specs=pl.BlockSpec(
                (1, 2, rows, half * rows), lambda b, at: (b + first_bin, 0, 0, at[0])
            ),
            scratch_shapes=scratch,
        ),
        out_shape=jax.ShapeDtypeStruct((all_bins, 2, rows, chan * rows), jnp.float32),
        input_output_aliases={2 + len(others): 0} if bases else {},
        compiler_params=pltpu.CompilerParams(vmem_limit_bytes=56 * 1024 * 1024),
        cost_estimate=pl.CostEstimate(
            flops=4 * bins * rows * half * rows * segments * lanes,
            bytes_accessed=bins * half * rows * (2 * segments * lanes + 8 * rows),
            transcendentals=0,
        ),
        name="cross",
    )(place, own, *others, *bases)


def chan_index(x, z, c):
    return x * 8 + z * 2 + c


PLACES = [(x, z, c) for x in range(2) for z in range(4) for c in range(2)]
ACROSS = [(chan_index(x, z, c), chan_index(1 - x, z, c)) for x, z, c in PLACES]
SIBLING = [(chan_index(x, z, c), chan_index(x, z, 1 - c)) for x, z, c in PLACES]
X_HALVES = [list(range(8)), list(range(8, 16))]


def send(value, pairs):
    return lax.ppermute(value, "chan", pairs)


def gather(value):
    return lax.all_gather(value, "chan", axis_index_groups=X_HALVES)


def exchange(value):
    return lax.all_to_all(value, "seg", split_axis=0, concat_axis=0, tiled=True)


FIRST = 7


def local(strain_rate, window_starts):
    segments = lax.axis_size("seg")
    chan = lax.axis_size("chan")
    bins = F // segments
    spectra_b, spectra_a = local_spectra(strain_rate, window_starts, segments, FIRST)
    me = lax.axis_index("chan")
    z = lax.rem(me // 2, 4)
    core = lax.rem(me, 2)
    near = jnp.stack([me // 8, z, core])
    far = jnp.stack([1 - me // 8, z, core])

    count = segments * window_starts.shape[0]
    stacked = functools.partial(cross, all_bins=bins, chan=chan, window_count=count)

    own_b = exchange(spectra_b)
    all_b = gather(own_b)
    far_b = [send(own_b, ACROSS)]
    own_a = after(exchange(spectra_a), far_b[0])
    far_a = send(own_a, ACROSS)
    all_a = gather(own_a)
    all_far_a = gather(far_a)
    for hop in range(1, 4):
        at = lax.rem(z + hop, 4) * 2 + core
        far_b.append(send(lax.dynamic_index_in_dim(all_b, at, 0, keepdims=False), ACROSS))
    out = stacked(after(near, far_b[1]), own_b, all_b, None, 0)
    out = stacked(near, own_a, all_a, out, FIRST)
    out, last = together(out, far_b[3])
    far_b = far_b + [send(p, SIBLING) for p in (*far_b[:3], last)]
    out = stacked(far, own_b, far_b, out, 0)
    return stacked(far, own_a, all_far_a, out, FIRST)


def solution(mesh):
    in_specs = (P("chan", "seg"), P("seg"))
    out_specs = P("seg", None, "chan", None)
    return jax.shard_map(local, mesh=mesh, in_specs=in_specs, out_specs=out_specs, check_vma=False)
```

```python
import functools
import math

import jax
import jax.numpy as jnp
import numpy as np
from jax import lax
from jax.experimental import pallas as pl
from jax.experimental.pallas import tpu as pltpu
from jax.sharding import PartitionSpec as P
import ml_dtypes

WIN = 1024
QUARTER = WIN // 4
F = 96
K0 = 10
EPSILON = 1e-06
CLIP_LEVEL = 1.5
LANES = 128
GROUP = 32
BATCH = 16
STRIDE = 40


def fourier_columns():
    n = np.arange(WIN, dtype=np.int64)
    k = K0 + np.arange(F, dtype=np.int64)
    m = (n[:, None] * k[None, :]) % WIN
    phase = (m.astype(np.float32) * np.float32(2.0 * math.pi / WIN)).astype(np.float64)
    table = np.zeros((WIN, 2 * LANES), np.float32)
    table[:, :F] = np.cos(phase)
    table[:, LANES : LANES + F] = -np.sin(phase)
    return table.astype(ml_dtypes.bfloat16)


def hann_row():
    phase = (np.arange(WIN, dtype=np.float32) * np.float32(2.0 * math.pi / WIN)).astype(np.float64)
    return (0.5 - 0.5 * np.cos(phase)).astype(np.float32)[None, :]


def spectra_kernel(starts, samples, table, hann, out_b, out_a, taps, real, imag, staged):
    group = samples.shape[0]
    windows = starts.shape[0]

    def some_windows(i, _):
        for k in range(BATCH):
            first = pl.multiple_of(starts[i * BATCH + k] * QUARTER, QUARTER)
            win = samples[:, pl.ds(first, WIN)].astype(jnp.float32)
            power = jnp.sum(win * win, -1, keepdims=True) * (1.0 / WIN)
            level = CLIP_LEVEL * jnp.sqrt(power + EPSILON)
            tap = jnp.clip(win, -level, level) * hann[...]
            taps[k * group : (k + 1) * group, :] = tap.astype(jnp.bfloat16)
        spec = jnp.dot(taps[...], table[...], preferred_element_type=jnp.float32)
        for k in range(BATCH):
            at = pl.ds(pl.multiple_of((i * BATCH + k) * STRIDE, 8), group)
            real[at, :] = spec[k * group : (k + 1) * group, :LANES]
            imag[at, :] = spec[k * group : (k + 1) * group, LANES:]
        return 0

    lax.fori_loop(0, windows // BATCH, some_windows, 0)

    def one_channel(c, _):
        at = pl.ds(c, windows, stride=STRIDE)
        both = jnp.concatenate([real[at, :], imag[at, :]], 0)
        turned = both.T[:F]
        total = jnp.sum(turned * turned, 0, keepdims=True)
        total = total + pltpu.roll(total, windows, 1)
        scale = lax.rsqrt(total * (1.0 / (2 * F)) + EPSILON)
        staged[pl.ds(c, F, stride=STRIDE), :] = turned * scale
        return 0

    lax.fori_loop(0, group, one_channel, 0, unroll=16)

    segments, first = out_b.shape[:2]
    bins = F // segments
    for s in range(segments):
        for b in range(bins):
            value = staged[pl.ds((s * bins + b) * STRIDE, group), :].astype(jnp.bfloat16)
            if b < first:
                out_b[s, b] = value
            else:
                out_a[s, b - first] = value


def local_spectra(samples, starts, segments, first):
    channels, length = samples.shape
    windows = starts.shape[0]
    counts = (first, F // segments - first)
    return pl.pallas_call(
        spectra_kernel,
        grid=(channels // GROUP,),
        in_specs=[
            pl.BlockSpec(memory_space=pltpu.SMEM),
            pl.BlockSpec((GROUP, length), lambda g: (g, 0)),
            pl.BlockSpec((WIN, 2 * LANES), lambda g: (0, 0)),
            pl.BlockSpec((1, WIN), lambda g: (0, 0)),
        ],
        out_specs=[
            pl.BlockSpec((segments, n, GROUP, LANES), lambda g: (0, 0, g, 0)) for n in counts
        ],
        out_shape=[
            jax.ShapeDtypeStruct((segments, n, channels, LANES), jnp.bfloat16) for n in counts
        ],
        scratch_shapes=[
            pltpu.VMEM((BATCH * GROUP, WIN), jnp.bfloat16),
            pltpu.VMEM((windows * STRIDE, LANES), jnp.float32),
            pltpu.VMEM((windows * STRIDE, LANES), jnp.float32),
            pltpu.VMEM((F * STRIDE, LANES), jnp.float32),
        ],
        compiler_params=pltpu.CompilerParams(vmem_limit_bytes=48 * 1024 * 1024),
        name="spectra",
    )(starts, samples, jnp.asarray(fourier_columns()), jnp.asarray(hann_row()))


def rotated(own):
    parts = []
    for s in range(own.shape[1] // LANES):
        tile = own[:, s * LANES : (s + 1) * LANES].astype(jnp.float32)
        lane = lax.broadcasted_iota(jnp.int32, tile.shape, 1)
        tile = pltpu.roll(tile, LANES // 2, 1)
        parts.append(jnp.where(lane < LANES // 2, tile, -tile).astype(jnp.bfloat16))
    return jnp.concatenate(parts, 1)


def after_kernel(*refs):
    del refs


def together(*values):
    return pl.pallas_call(
        after_kernel,
        in_specs=[pl.BlockSpec(memory_space=pl.ANY)] * len(values),
        out_specs=[pl.BlockSpec(memory_space=pl.ANY)] * len(values),
        out_shape=[jax.ShapeDtypeStruct(v.shape, v.dtype) for v in values],
        input_output_aliases={i: i for i in range(len(values))},
        name="together",
    )(*values)


def after(value, *first):
    return pl.pallas_call(
        after_kernel,
        in_specs=[pl.BlockSpec(memory_space=pl.ANY)] * (1 + len(first)),
        out_specs=pl.BlockSpec(memory_space=pl.ANY),
        out_shape=jax.ShapeDtypeStruct(value.shape, value.dtype),
        input_output_aliases={0: 0},
        name="after",
    )(value, *first)


def stack(scale, own, right):
    segments, rows = own.shape[0], own.shape[2]
    mine = jnp.concatenate([own[s, 0] for s in range(segments)], 1)
    left = jnp.concatenate([mine, rotated(mine)], 0)
    acc = lax.dot_general(left, right, (((1,), (1,)), ((), ())), preferred_element_type=jnp.float32)
    return (acc * scale).reshape(2, rows, acc.shape[1])


def gathered_kernel(scale, place, own, others, *refs):
    del place
    segments = own.shape[0]
    columns = others.shape[0] * others.shape[3]
    right = [others[:, s, 0].reshape(columns, LANES) for s in range(segments)]
    refs[-1][0] = stack(scale, own, jnp.concatenate(right, 1))


def pieces_kernel(scale, place, own, *refs):
    pieces = refs[:8]
    out, buf, sems = refs[-3:]
    step = pl.program_id(0)
    z, core = place[1], place[2]

    def copies(b, slot):
        made = []
        for c in range(2):
            for i in range(4):
                at = lax.rem(z + i, 4) * 2 + (core if c == 0 else 1 - core)
                made.append(
                    pltpu.make_async_copy(
                        pieces[4 * c + i].at[:, b], buf.at[slot, at], sems.at[slot, 4 * c + i]
                    )
                )
        return made

    slot = lax.rem(step, 2)

    @pl.when(step == 0)
    def _():
        for copy in copies(0, 0):
            copy.start()

    @pl.when(step + 1 < pl.num_programs(0))
    def _():
        for copy in copies(step + 1, 1 - slot):
            copy.start()

    for copy in copies(step, slot):
        copy.wait()

    segments = own.shape[0]
    columns = buf.shape[1] * buf.shape[3]
    right = [buf[slot, :, s].reshape(columns, LANES) for s in range(segments)]
    out[0] = stack(scale, own, jnp.concatenate(right, 1))


def cross(place, own, others, base, first_bin, *, all_bins, chan, window_count):
    segments, bins, rows, lanes = own.shape
    half = chan // 2
    bases = [] if base is None else [base]
    anywhere = pl.BlockSpec(memory_space=pl.ANY)
    if isinstance(others, list):
        kernel = pieces_kernel
        specs = [anywhere] * len(others)
        scratch = [
            pltpu.VMEM((2, half, segments, rows, lanes), own.dtype),
            pltpu.SemaphoreType.DMA((2, len(others))),
        ]
    else:
        kernel = gathered_kernel
        specs = [pl.BlockSpec((half, segments, 1, rows, lanes), lambda b, at: (0, 0, b, 0, 0))]
        others = [others]
        scratch = []
    return pl.pallas_call(
        functools.partial(kernel, 1.0 / window_count),
        grid_spec=pltpu.PrefetchScalarGridSpec(
            num_scalar_prefetch=1,
            grid=(bins,),
            in_specs=[pl.BlockSpec((segments, 1, rows, lanes), lambda b, at: (0, b, 0, 0))]
            + specs
            + [anywhere] * len(bases),
            out_specs=pl.BlockSpec(
                (1, 2, rows, half * rows), lambda b, at: (b + first_bin, 0, 0, at[0])
            ),
            scratch_shapes=scratch,
        ),
        out_shape=jax.ShapeDtypeStruct((all_bins, 2, rows, chan * rows), jnp.float32),
        input_output_aliases={2 + len(others): 0} if bases else {},
        compiler_params=pltpu.CompilerParams(vmem_limit_bytes=56 * 1024 * 1024),
        cost_estimate=pl.CostEstimate(
            flops=4 * bins * rows * half * rows * segments * lanes,
            bytes_accessed=bins * half * rows * (2 * segments * lanes + 8 * rows),
            transcendentals=0,
        ),
        name="cross",
    )(place, own, *others, *bases)


def chan_index(x, z, c):
    return x * 8 + z * 2 + c


PLACES = [(x, z, c) for x in range(2) for z in range(4) for c in range(2)]
ACROSS = [(chan_index(x, z, c), chan_index(1 - x, z, c)) for x, z, c in PLACES]
SIBLING = [(chan_index(x, z, c), chan_index(x, z, 1 - c)) for x, z, c in PLACES]
X_HALVES = [list(range(8)), list(range(8, 16))]


def send(value, pairs):
    return lax.ppermute(value, "chan", pairs)


def gather(value):
    return lax.all_gather(value, "chan", axis_index_groups=X_HALVES)


def exchange(value):
    return lax.all_to_all(value, "seg", split_axis=0, concat_axis=0, tiled=True)


FIRST = 6


def local(strain_rate, window_starts):
    segments = lax.axis_size("seg")
    chan = lax.axis_size("chan")
    bins = F // segments
    spectra_b, spectra_a = local_spectra(strain_rate, window_starts, segments, FIRST)
    me = lax.axis_index("chan")
    z = lax.rem(me // 2, 4)
    core = lax.rem(me, 2)
    near = jnp.stack([me // 8, z, core])
    far = jnp.stack([1 - me // 8, z, core])

    count = segments * window_starts.shape[0]
    stacked = functools.partial(cross, all_bins=bins, chan=chan, window_count=count)

    own_b = exchange(spectra_b)
    all_b = gather(own_b)
    far_b = [send(own_b, ACROSS)]
    own_a = after(exchange(spectra_a), far_b[0])
    far_a = send(own_a, ACROSS)
    all_a = gather(own_a)
    all_far_a = gather(far_a)
    for hop in range(1, 4):
        at = lax.rem(z + hop, 4) * 2 + core
        far_b.append(send(lax.dynamic_index_in_dim(all_b, at, 0, keepdims=False), ACROSS))
    out = stacked(after(near, far_b[1]), own_b, all_b, None, 0)
    out = stacked(near, own_a, all_a, out, FIRST)
    out, last = together(out, far_b[3])
    far_b = far_b + [send(p, SIBLING) for p in (*far_b[:3], last)]
    out = stacked(far, own_b, far_b, out, 0)
    return stacked(far, own_a, all_far_a, out, FIRST)


def solution(mesh):
    in_specs = (P("chan", "seg"), P("seg"))
    out_specs = P("seg", None, "chan", None)
    return jax.shard_map(local, mesh=mesh, in_specs=in_specs, out_specs=out_specs, check_vma=False)
```

```python
import functools
import math

import jax
import jax.numpy as jnp
import numpy as np
from jax import lax
from jax.experimental import pallas as pl
from jax.experimental.pallas import tpu as pltpu
from jax.sharding import PartitionSpec as P
import ml_dtypes

WIN = 1024
QUARTER = WIN // 4
F = 96
K0 = 10
EPSILON = 1e-06
CLIP_LEVEL = 1.5
LANES = 128
GROUP = 32
BATCH = 16
STRIDE = 40


def fourier_columns():
    n = np.arange(WIN, dtype=np.int64)
    k = K0 + np.arange(F, dtype=np.int64)
    m = (n[:, None] * k[None, :]) % WIN
    phase = (m.astype(np.float32) * np.float32(2.0 * math.pi / WIN)).astype(np.float64)
    table = np.zeros((WIN, 2 * LANES), np.float32)
    table[:, :F] = np.cos(phase)
    table[:, LANES : LANES + F] = -np.sin(phase)
    return table.astype(ml_dtypes.bfloat16)


def hann_row():
    phase = (np.arange(WIN, dtype=np.float32) * np.float32(2.0 * math.pi / WIN)).astype(np.float64)
    return (0.5 - 0.5 * np.cos(phase)).astype(np.float32)[None, :]


def spectra_kernel(starts, samples, table, hann, out_b, out_a, taps, real, imag, staged):
    group = samples.shape[0]
    windows = starts.shape[0]

    def some_windows(i, _):
        for k in range(BATCH):
            first = pl.multiple_of(starts[i * BATCH + k] * QUARTER, QUARTER)
            win = samples[:, pl.ds(first, WIN)].astype(jnp.float32)
            power = jnp.sum(win * win, -1, keepdims=True) * (1.0 / WIN)
            level = CLIP_LEVEL * jnp.sqrt(power + EPSILON)
            tap = jnp.clip(win, -level, level) * hann[...]
            taps[k * group : (k + 1) * group, :] = tap.astype(jnp.bfloat16)
        spec = jnp.dot(taps[...], table[...], preferred_element_type=jnp.float32)
        for k in range(BATCH):
            at = pl.ds(pl.multiple_of((i * BATCH + k) * STRIDE, 8), group)
            real[at, :] = spec[k * group : (k + 1) * group, :LANES]
            imag[at, :] = spec[k * group : (k + 1) * group, LANES:]
        return 0

    lax.fori_loop(0, windows // BATCH, some_windows, 0)

    def one_channel(c, _):
        at = pl.ds(c, windows, stride=STRIDE)
        both = jnp.concatenate([real[at, :], imag[at, :]], 0)
        turned = both.T[:F]
        total = jnp.sum(turned * turned, 0, keepdims=True)
        total = total + pltpu.roll(total, windows, 1)
        scale = lax.rsqrt(total * (1.0 / (2 * F)) + EPSILON)
        staged[pl.ds(c, F, stride=STRIDE), :] = turned * scale
        return 0

    lax.fori_loop(0, group, one_channel, 0, unroll=16)

    segments, first = out_b.shape[:2]
    bins = F // segments
    for s in range(segments):
        for b in range(bins):
            value = staged[pl.ds((s * bins + b) * STRIDE, group), :].astype(jnp.bfloat16)
            if b < first:
                out_b[s, b] = value
            else:
                out_a[s, b - first] = value


def local_spectra(samples, starts, segments, first):
    channels, length = samples.shape
    windows = starts.shape[0]
    counts = (first, F // segments - first)
    return pl.pallas_call(
        spectra_kernel,
        grid=(channels // GROUP,),
        in_specs=[
            pl.BlockSpec(memory_space=pltpu.SMEM),
            pl.BlockSpec((GROUP, length), lambda g: (g, 0)),
            pl.BlockSpec((WIN, 2 * LANES), lambda g: (0, 0)),
            pl.BlockSpec((1, WIN), lambda g: (0, 0)),
        ],
        out_specs=[
            pl.BlockSpec((segments, n, GROUP, LANES), lambda g: (0, 0, g, 0)) for n in counts
        ],
        out_shape=[
            jax.ShapeDtypeStruct((segments, n, channels, LANES), jnp.bfloat16) for n in counts
        ],
        scratch_shapes=[
            pltpu.VMEM((BATCH * GROUP, WIN), jnp.bfloat16),
            pltpu.VMEM((windows * STRIDE, LANES), jnp.float32),
            pltpu.VMEM((windows * STRIDE, LANES), jnp.float32),
            pltpu.VMEM((F * STRIDE, LANES), jnp.float32),
        ],
        compiler_params=pltpu.CompilerParams(vmem_limit_bytes=48 * 1024 * 1024),
        name="spectra",
    )(starts, samples, jnp.asarray(fourier_columns()), jnp.asarray(hann_row()))


def rotated(own):
    parts = []
    for s in range(own.shape[1] // LANES):
        tile = own[:, s * LANES : (s + 1) * LANES].astype(jnp.float32)
        lane = lax.broadcasted_iota(jnp.int32, tile.shape, 1)
        tile = pltpu.roll(tile, LANES // 2, 1)
        parts.append(jnp.where(lane < LANES // 2, tile, -tile).astype(jnp.bfloat16))
    return jnp.concatenate(parts, 1)


def after_kernel(*refs):
    del refs


def after(first, *values):
    anywhere = pl.BlockSpec(memory_space=pl.ANY)
    return pl.pallas_call(
        after_kernel,
        in_specs=[anywhere] * (len(values) + len(first)),
        out_specs=[anywhere] * len(values),
        out_shape=[jax.ShapeDtypeStruct(v.shape, v.dtype) for v in values],
        input_output_aliases={i: i for i in range(len(values))},
        name="after",
    )(*values, *first)


def stack(scale, own, right):
    segments, rows = own.shape[0], own.shape[2]
    mine = jnp.concatenate([own[s, 0] for s in range(segments)], 1)
    left = jnp.concatenate([mine, rotated(mine)], 0)
    acc = lax.dot_general(left, right, (((1,), (1,)), ((), ())), preferred_element_type=jnp.float32)
    return (acc * scale).reshape(2, rows, acc.shape[1])


def gathered_kernel(scale, place, own, others, *refs):
    del place
    segments = own.shape[0]
    columns = others.shape[0] * others.shape[3]
    right = [others[:, s, 0].reshape(columns, LANES) for s in range(segments)]
    refs[-1][0] = stack(scale, own, jnp.concatenate(right, 1))


def pieces_kernel(scale, hops, place, own, *refs):
    count = len(hops)
    pieces = refs[: 2 * count]
    out, buf, sems = refs[-3:]
    step = pl.program_id(0)
    z, core = place[1], place[2]

    def copies(b, slot):
        made = []
        for c in range(2):
            for i, (hop, start) in enumerate(hops):
                piece = pieces[count * c + i].at[:, b]
                at = lax.rem(z + hop, 4) * 2 + (core if c == 0 else 1 - core)
                to = buf.at[slot, at, pl.ds(start, piece.shape[0])]
                made.append(pltpu.make_async_copy(piece, to, sems.at[slot, count * c + i]))
        return made

    slot = lax.rem(step, 2)

    @pl.when(step == 0)
    def _():
        for copy in copies(0, 0):
            copy.start()

    @pl.when(step + 1 < pl.num_programs(0))
    def _():
        for copy in copies(step + 1, 1 - slot):
            copy.start()

    for copy in copies(step, slot):
        copy.wait()

    segments = own.shape[0]
    columns = buf.shape[1] * buf.shape[3]
    right = [buf[slot, :, s].reshape(columns, LANES) for s in range(segments)]
    out[0] = stack(scale, own, jnp.concatenate(right, 1))


def cross(place, own, others, base, first_bin, hops=None, *, all_bins, chan, window_count):
    segments, bins, rows, lanes = own.shape
    half = chan // 2
    bases = [] if base is None else [base]
    anywhere = pl.BlockSpec(memory_space=pl.ANY)
    if isinstance(others, list):
        kernel = functools.partial(pieces_kernel, 1.0 / window_count, hops)
        specs = [anywhere] * len(others)
        scratch = [
            pltpu.VMEM((2, half, segments, rows, lanes), own.dtype),
            pltpu.SemaphoreType.DMA((2, len(others))),
        ]
    else:
        kernel = functools.partial(gathered_kernel, 1.0 / window_count)
        specs = [pl.BlockSpec((half, segments, 1, rows, lanes), lambda b, at: (0, 0, b, 0, 0))]
        others = [others]
        scratch = []
    return pl.pallas_call(
        kernel,
        grid_spec=pltpu.PrefetchScalarGridSpec(
            num_scalar_prefetch=1,
            grid=(bins,),
            in_specs=[pl.BlockSpec((segments, 1, rows, lanes), lambda b, at: (0, b, 0, 0))]
            + specs
            + [anywhere] * len(bases),
            out_specs=pl.BlockSpec(
                (1, 2, rows, half * rows), lambda b, at: (b + first_bin, 0, 0, at[0])
            ),
            scratch_shapes=scratch,
        ),
        out_shape=jax.ShapeDtypeStruct((all_bins, 2, rows, chan * rows), jnp.float32),
        input_output_aliases={2 + len(others): 0} if bases else {},
        compiler_params=pltpu.CompilerParams(vmem_limit_bytes=56 * 1024 * 1024),
        cost_estimate=pl.CostEstimate(
            flops=4 * bins * rows * half * rows * segments * lanes,
            bytes_accessed=bins * half * rows * (2 * segments * lanes + 8 * rows),
            transcendentals=0,
        ),
        name="cross",
    )(place, own, *others, *bases)


def chan_index(x, z, c):
    return x * 8 + z * 2 + c


PLACES = [(x, z, c) for x in range(2) for z in range(4) for c in range(2)]
UP = [(chan_index(x, z, c), chan_index(x, (z + 1) % 4, c)) for x, z, c in PLACES]
DOWN = [(chan_index(x, z, c), chan_index(x, (z + 3) % 4, c)) for x, z, c in PLACES]
ACROSS = [(chan_index(x, z, c), chan_index(1 - x, z, c)) for x, z, c in PLACES]
SIBLING = [(chan_index(x, z, c), chan_index(x, z, 1 - c)) for x, z, c in PLACES]
X_HALVES = [list(range(8)), list(range(8, 16))]


def send(value, pairs):
    return lax.ppermute(value, "chan", pairs)


def gather(value):
    return lax.all_gather(value, "chan", axis_index_groups=X_HALVES)


def exchange(value):
    return lax.all_to_all(value, "seg", split_axis=0, concat_axis=0, tiled=True)


FIRST = 6
SPLIT = 4


def local(strain_rate, window_starts):
    segments = lax.axis_size("seg")
    chan = lax.axis_size("chan")
    bins = F // segments
    spectra_b, spectra_a = local_spectra(strain_rate, window_starts, segments, FIRST)
    me = lax.axis_index("chan")
    z = lax.rem(me // 2, 4)
    core = lax.rem(me, 2)
    near = jnp.stack([me // 8, z, core])
    far = jnp.stack([1 - me // 8, z, core])

    count = segments * window_starts.shape[0]
    stacked = functools.partial(cross, all_bins=bins, chan=chan, window_count=count)

    half = segments // 2
    ring = [(0, 0), (3, 0), (1, 0), (2, 0), (2, half)]

    own_b = exchange(spectra_b)
    all_b = gather(own_b)
    far_b = [send(own_b, ACROSS)]
    (own_a,) = after([far_b[0]], exchange(spectra_a))
    own_a1, own_a2 = own_a[:, :SPLIT], own_a[:, SPLIT:]
    x_a = send(own_a, ACROSS)
    all_a1 = gather(own_a1)
    up_a2, down_a2 = send(own_a2, UP), send(own_a2, DOWN)
    hops = [
        lax.dynamic_index_in_dim(all_b, lax.rem(z + hop, 4) * 2 + core, 0, keepdims=False)
        for hop in range(1, 4)
    ]
    x_a, *hops = after([], x_a, *hops)
    all_xa = gather(x_a)
    far_b = far_b + [send(hop, ACROSS) for hop in hops]
    near_a2 = [own_a2, up_a2, down_a2, send(up_a2[:half], UP), send(down_a2[half:], DOWN)]
    near_a2 = near_a2 + [send(p, SIBLING) for p in near_a2]

    (near,) = after([far_b[1]], near)
    out = stacked(near, own_b, all_b, None, 0)
    out = stacked(near, own_a1, all_a1, out, FIRST)
    out = stacked(near, own_a2, near_a2, out, FIRST + SPLIT, ring)
    out, last = after([], out, far_b[3])
    far_b[3] = last
    far_b = far_b + [send(p, SIBLING) for p in far_b]
    out = stacked(far, own_b, far_b, out, 0, [(0, 0), (1, 0), (2, 0), (3, 0)])
    return stacked(far, own_a, all_xa, out, FIRST)


def solution(mesh):
    in_specs = (P("chan", "seg"), P("seg"))
    out_specs = P("seg", None, "chan", None)
    return jax.shard_map(local, mesh=mesh, in_specs=in_specs, out_specs=out_specs, check_vma=False)
```

```python
import functools
import math

import jax
import jax.numpy as jnp
import numpy as np
from jax import lax
from jax.experimental import pallas as pl
from jax.experimental.pallas import tpu as pltpu
from jax.sharding import PartitionSpec as P
import ml_dtypes

WIN = 1024
QUARTER = WIN // 4
F = 96
K0 = 10
EPSILON = 1e-06
CLIP_LEVEL = 1.5
LANES = 128
GROUP = 32
BATCH = 16
STRIDE = 40


def fourier_columns():
    n = np.arange(WIN, dtype=np.int64)
    k = K0 + np.arange(F, dtype=np.int64)
    m = (n[:, None] * k[None, :]) % WIN
    phase = (m.astype(np.float32) * np.float32(2.0 * math.pi / WIN)).astype(np.float64)
    table = np.zeros((WIN, 2 * LANES), np.float32)
    table[:, :F] = np.cos(phase)
    table[:, LANES : LANES + F] = -np.sin(phase)
    return table.astype(ml_dtypes.bfloat16)


def hann_row():
    phase = (np.arange(WIN, dtype=np.float32) * np.float32(2.0 * math.pi / WIN)).astype(np.float64)
    return (0.5 - 0.5 * np.cos(phase)).astype(np.float32)[None, :]


def spectra_kernel(starts, samples, table, hann, out_b, out_a, taps, real, imag, staged):
    group = samples.shape[0]
    windows = starts.shape[0]

    def some_windows(i, _):
        for k in range(BATCH):
            first = pl.multiple_of(starts[i * BATCH + k] * QUARTER, QUARTER)
            win = samples[:, pl.ds(first, WIN)].astype(jnp.float32)
            power = jnp.sum(win * win, -1, keepdims=True) * (1.0 / WIN)
            level = CLIP_LEVEL * jnp.sqrt(power + EPSILON)
            tap = jnp.clip(win, -level, level) * hann[...]
            taps[k * group : (k + 1) * group, :] = tap.astype(jnp.bfloat16)
        spec = jnp.dot(taps[...], table[...], preferred_element_type=jnp.float32)
        for k in range(BATCH):
            at = pl.ds(pl.multiple_of((i * BATCH + k) * STRIDE, 8), group)
            real[at, :] = spec[k * group : (k + 1) * group, :LANES]
            imag[at, :] = spec[k * group : (k + 1) * group, LANES:]
        return 0

    lax.fori_loop(0, windows // BATCH, some_windows, 0)

    def one_channel(c, _):
        at = pl.ds(c, windows, stride=STRIDE)
        both = jnp.concatenate([real[at, :], imag[at, :]], 0)
        turned = both.T[:F]
        total = jnp.sum(turned * turned, 0, keepdims=True)
        total = total + pltpu.roll(total, windows, 1)
        scale = lax.rsqrt(total * (1.0 / (2 * F)) + EPSILON)
        staged[pl.ds(c, F, stride=STRIDE), :] = turned * scale
        return 0

    lax.fori_loop(0, group, one_channel, 0, unroll=16)

    segments, first = out_b.shape[:2]
    bins = F // segments
    for s in range(segments):
        for b in range(bins):
            value = staged[pl.ds((s * bins + b) * STRIDE, group), :].astype(jnp.bfloat16)
            if b < first:
                out_b[s, b] = value
            else:
                out_a[s, b - first] = value


def local_spectra(samples, starts, segments, first):
    channels, length = samples.shape
    windows = starts.shape[0]
    counts = (first, F // segments - first)
    return pl.pallas_call(
        spectra_kernel,
        grid=(channels // GROUP,),
        in_specs=[
            pl.BlockSpec(memory_space=pltpu.SMEM),
            pl.BlockSpec((GROUP, length), lambda g: (g, 0)),
            pl.BlockSpec((WIN, 2 * LANES), lambda g: (0, 0)),
            pl.BlockSpec((1, WIN), lambda g: (0, 0)),
        ],
        out_specs=[
            pl.BlockSpec((segments, n, GROUP, LANES), lambda g: (0, 0, g, 0)) for n in counts
        ],
        out_shape=[
            jax.ShapeDtypeStruct((segments, n, channels, LANES), jnp.bfloat16) for n in counts
        ],
        scratch_shapes=[
            pltpu.VMEM((BATCH * GROUP, WIN), jnp.bfloat16),
            pltpu.VMEM((windows * STRIDE, LANES), jnp.float32),
            pltpu.VMEM((windows * STRIDE, LANES), jnp.float32),
            pltpu.VMEM((F * STRIDE, LANES), jnp.float32),
        ],
        compiler_params=pltpu.CompilerParams(vmem_limit_bytes=48 * 1024 * 1024),
        name="spectra",
    )(starts, samples, jnp.asarray(fourier_columns()), jnp.asarray(hann_row()))


def rotated(own):
    parts = []
    for s in range(own.shape[1] // LANES):
        tile = own[:, s * LANES : (s + 1) * LANES].astype(jnp.float32)
        lane = lax.broadcasted_iota(jnp.int32, tile.shape, 1)
        tile = pltpu.roll(tile, LANES // 2, 1)
        parts.append(jnp.where(lane < LANES // 2, tile, -tile).astype(jnp.bfloat16))
    return jnp.concatenate(parts, 1)


def after_kernel(*refs):
    del refs


def after(first, *values):
    anywhere = pl.BlockSpec(memory_space=pl.ANY)
    return pl.pallas_call(
        after_kernel,
        in_specs=[anywhere] * (len(values) + len(first)),
        out_specs=[anywhere] * len(values),
        out_shape=[jax.ShapeDtypeStruct(v.shape, v.dtype) for v in values],
        input_output_aliases={i: i for i in range(len(values))},
        name="after",
    )(*values, *first)


def stack(scale, own, right):
    segments, rows = own.shape[0], own.shape[2]
    mine = jnp.concatenate([own[s, 0] for s in range(segments)], 1)
    left = jnp.concatenate([mine, rotated(mine)], 0)
    acc = lax.dot_general(left, right, (((1,), (1,)), ((), ())), preferred_element_type=jnp.float32)
    return (acc * scale).reshape(2, rows, acc.shape[1])


def cross_kernel(scale, hops, place, own, *refs):
    out, buf, sems = refs[-3:]
    step = pl.program_id(0)
    steps = pl.num_programs(0)
    slots = buf.shape[0]
    z, core = place[1], place[2]

    def copies(b):
        slot = lax.rem(b, slots)
        made = []
        if hops is None:
            for i in range(buf.shape[1]):
                made.append((refs[0].at[i, :, b], buf.at[slot, i]))
        else:
            for c in range(2):
                for i, (hop, start) in enumerate(hops):
                    piece = refs[len(hops) * c + i].at[:, b]
                    at = lax.rem(z + hop, 4) * 2 + (core if c == 0 else 1 - core)
                    made.append((piece, buf.at[slot, at, pl.ds(start, piece.shape[0])]))
        return [
            pltpu.make_async_copy(piece, to, sems.at[slot, i]) for i, (piece, to) in enumerate(made)
        ]

    @pl.when(step == 0)
    def _():
        for copy in copies(0):
            copy.start()

    for ahead in range(1, slots - 1):

        @pl.when((step == 0) & (ahead < steps))
        def _():
            for copy in copies(ahead):
                copy.start()

    @pl.when(step + slots - 1 < steps)
    def _():
        for copy in copies(step + slots - 1):
            copy.start()

    for copy in copies(step):
        copy.wait()

    slot = lax.rem(step, slots)
    segments = own.shape[0]
    columns = buf.shape[1] * buf.shape[3]
    right = [buf[slot, :, s].reshape(columns, LANES) for s in range(segments)]
    out[0] = stack(scale, own, jnp.concatenate(right, 1))


def cross(place, own, others, base, first_bin, hops=None, *, all_bins, chan, window_count):
    segments, bins, rows, lanes = own.shape
    half = chan // 2
    bases = [] if base is None else [base]
    anywhere = pl.BlockSpec(memory_space=pl.ANY)
    if not isinstance(others, list):
        others = [others]
    copies = half if hops is None else len(others)
    return pl.pallas_call(
        functools.partial(cross_kernel, 1.0 / window_count, hops),
        grid_spec=pltpu.PrefetchScalarGridSpec(
            num_scalar_prefetch=1,
            grid=(bins,),
            in_specs=[pl.BlockSpec((segments, 1, rows, lanes), lambda b, at: (0, b, 0, 0))]
            + [anywhere] * (len(others) + len(bases)),
            out_specs=pl.BlockSpec(
                (1, 2, rows, half * rows), lambda b, at: (b + first_bin, 0, 0, at[0])
            ),
            scratch_shapes=[
                pltpu.VMEM((SLOTS, half, segments, rows, lanes), own.dtype),
                pltpu.SemaphoreType.DMA((SLOTS, copies)),
            ],
        ),
        out_shape=jax.ShapeDtypeStruct((all_bins, 2, rows, chan * rows), jnp.float32),
        input_output_aliases={2 + len(others): 0} if bases else {},
        compiler_params=pltpu.CompilerParams(vmem_limit_bytes=56 * 1024 * 1024),
        cost_estimate=pl.CostEstimate(
            flops=4 * bins * rows * half * rows * segments * lanes,
            bytes_accessed=bins * half * rows * (2 * segments * lanes + 8 * rows),
            transcendentals=0,
        ),
        name="cross",
    )(place, own, *others, *bases)


def chan_index(x, z, c):
    return x * 8 + z * 2 + c


PLACES = [(x, z, c) for x in range(2) for z in range(4) for c in range(2)]
UP = [(chan_index(x, z, c), chan_index(x, (z + 1) % 4, c)) for x, z, c in PLACES]
DOWN = [(chan_index(x, z, c), chan_index(x, (z + 3) % 4, c)) for x, z, c in PLACES]
ACROSS = [(chan_index(x, z, c), chan_index(1 - x, z, c)) for x, z, c in PLACES]
SIBLING = [(chan_index(x, z, c), chan_index(x, z, 1 - c)) for x, z, c in PLACES]
X_HALVES = [list(range(8)), list(range(8, 16))]


def send(value, pairs):
    return lax.ppermute(value, "chan", pairs)


def gather(value):
    return lax.all_gather(value, "chan", axis_index_groups=X_HALVES)


def exchange(value):
    return lax.all_to_all(value, "seg", split_axis=0, concat_axis=0, tiled=True)


FIRST = 5
SPLIT = 4
SLOTS = 3


def local(strain_rate, window_starts):
    segments = lax.axis_size("seg")
    chan = lax.axis_size("chan")
    bins = F // segments
    spectra_b, spectra_a = local_spectra(strain_rate, window_starts, segments, FIRST)
    me = lax.axis_index("chan")
    z = lax.rem(me // 2, 4)
    core = lax.rem(me, 2)
    near = jnp.stack([me // 8, z, core])
    far = jnp.stack([1 - me // 8, z, core])

    count = segments * window_starts.shape[0]
    stacked = functools.partial(cross, all_bins=bins, chan=chan, window_count=count)

    half = segments // 2
    ring = [(0, 0), (3, 0), (1, 0), (2, 0), (2, half)]

    own_b = exchange(spectra_b)
    all_b = gather(own_b)
    far_b = [send(own_b, ACROSS)]
    (own_a,) = after([far_b[0]], exchange(spectra_a))
    own_a1, own_a2 = own_a[:, :SPLIT], own_a[:, SPLIT:]
    x_a = send(own_a, ACROSS)
    all_a1 = gather(own_a1)
    up_a2, down_a2 = send(own_a2, UP), send(own_a2, DOWN)
    hops = [
        lax.dynamic_index_in_dim(all_b, lax.rem(z + hop, 4) * 2 + core, 0, keepdims=False)
        for hop in range(1, 4)
    ]
    x_a, *hops = after([], x_a, *hops)
    all_xa = gather(x_a)
    far_b = far_b + [send(hop, ACROSS) for hop in hops]
    near_a2 = [own_a2, up_a2, down_a2, send(up_a2[:half], UP), send(down_a2[half:], DOWN)]
    near_a2 = near_a2 + [send(p, SIBLING) for p in near_a2]

    (near,) = after([far_b[1]], near)
    out = stacked(near, own_b, all_b, None, 0)
    out = stacked(near, own_a1, all_a1, out, FIRST)
    out = stacked(near, own_a2, near_a2, out, FIRST + SPLIT, ring)
    out, last = after([], out, far_b[3])
    far_b[3] = last
    far_b = far_b + [send(p, SIBLING) for p in far_b]
    out = stacked(far, own_b, far_b, out, 0, [(0, 0), (1, 0), (2, 0), (3, 0)])
    return stacked(far, own_a, all_xa, out, FIRST)


def solution(mesh):
    in_specs = (P("chan", "seg"), P("seg"))
    out_specs = P("seg", None, "chan", None)
    return jax.shard_map(local, mesh=mesh, in_specs=in_specs, out_specs=out_specs, check_vma=False)
```

```python
import functools
import math

import jax
import jax.numpy as jnp
import numpy as np
from jax import lax
from jax.experimental import pallas as pl
from jax.experimental.pallas import tpu as pltpu
from jax.sharding import PartitionSpec as P
import ml_dtypes

WIN = 1024
QUARTER = WIN // 4
F = 96
K0 = 10
EPSILON = 1e-06
CLIP_LEVEL = 1.5
LANES = 128
GROUP = 48
BATCH = 16
STRIDE = 56


def fourier_columns():
    n = np.arange(WIN, dtype=np.int64)
    k = K0 + np.arange(F, dtype=np.int64)
    m = (n[:, None] * k[None, :]) % WIN
    phase = (m.astype(np.float32) * np.float32(2.0 * math.pi / WIN)).astype(np.float64)
    table = np.zeros((WIN, 2 * LANES), np.float32)
    table[:, :F] = np.cos(phase)
    table[:, LANES : LANES + F] = -np.sin(phase)
    return table.astype(ml_dtypes.bfloat16)


def hann_row():
    phase = (np.arange(WIN, dtype=np.float32) * np.float32(2.0 * math.pi / WIN)).astype(np.float64)
    return (0.5 - 0.5 * np.cos(phase)).astype(np.float32)[None, :]


def spectra_kernel(starts, samples, table, hann, out_b, out_a, taps, real, imag, staged):
    group = samples.shape[0]
    windows = starts.shape[0]

    def some_windows(i, _):
        for k in range(BATCH):
            first = pl.multiple_of(starts[i * BATCH + k] * QUARTER, QUARTER)
            win = samples[:, pl.ds(first, WIN)].astype(jnp.float32)
            power = jnp.sum(win * win, -1, keepdims=True) * (1.0 / WIN)
            level = CLIP_LEVEL * jnp.sqrt(power + EPSILON)
            tap = jnp.clip(win, -level, level) * hann[...]
            taps[k * group : (k + 1) * group, :] = tap.astype(jnp.bfloat16)
        spec = jnp.dot(taps[...], table[...], preferred_element_type=jnp.float32)
        for k in range(BATCH):
            at = pl.ds(pl.multiple_of((i * BATCH + k) * STRIDE, 8), group)
            real[at, :] = spec[k * group : (k + 1) * group, :LANES]
            imag[at, :] = spec[k * group : (k + 1) * group, LANES:]
        return 0

    lax.fori_loop(0, windows // BATCH, some_windows, 0)

    def one_channel(c, _):
        at = pl.ds(c, windows, stride=STRIDE)
        both = jnp.concatenate([real[at, :], imag[at, :]], 0)
        turned = both.T[:F]
        total = jnp.sum(turned * turned, 0, keepdims=True)
        total = total + pltpu.roll(total, windows, 1)
        scale = lax.rsqrt(total * (1.0 / (2 * F)) + EPSILON)
        staged[pl.ds(c, F, stride=STRIDE), :] = turned * scale
        return 0

    lax.fori_loop(0, group, one_channel, 0, unroll=16)

    segments, first = out_b.shape[:2]
    bins = F // segments
    for s in range(segments):
        for b in range(bins):
            value = staged[pl.ds((s * bins + b) * STRIDE, group), :].astype(jnp.bfloat16)
            if b < first:
                out_b[s, b] = value
            else:
                out_a[s, b - first] = value


def local_spectra(samples, starts, segments, first):
    channels, length = samples.shape
    windows = starts.shape[0]
    counts = (first, F // segments - first)
    return pl.pallas_call(
        spectra_kernel,
        grid=(channels // GROUP,),
        in_specs=[
            pl.BlockSpec(memory_space=pltpu.SMEM),
            pl.BlockSpec((GROUP, length), lambda g: (g, 0)),
            pl.BlockSpec((WIN, 2 * LANES), lambda g: (0, 0)),
            pl.BlockSpec((1, WIN), lambda g: (0, 0)),
        ],
        out_specs=[
            pl.BlockSpec((segments, n, GROUP, LANES), lambda g: (0, 0, g, 0)) for n in counts
        ],
        out_shape=[
            jax.ShapeDtypeStruct((segments, n, channels, LANES), jnp.bfloat16) for n in counts
        ],
        scratch_shapes=[
            pltpu.VMEM((BATCH * GROUP, WIN), jnp.bfloat16),
            pltpu.VMEM((windows * STRIDE, LANES), jnp.float32),
            pltpu.VMEM((windows * STRIDE, LANES), jnp.float32),
            pltpu.VMEM((F * STRIDE, LANES), jnp.float32),
        ],
        compiler_params=pltpu.CompilerParams(vmem_limit_bytes=48 * 1024 * 1024),
        name="spectra",
    )(starts, samples, jnp.asarray(fourier_columns()), jnp.asarray(hann_row()))


def rotated(own):
    parts = []
    for s in range(own.shape[1] // LANES):
        tile = own[:, s * LANES : (s + 1) * LANES].astype(jnp.float32)
        lane = lax.broadcasted_iota(jnp.int32, tile.shape, 1)
        tile = pltpu.roll(tile, LANES // 2, 1)
        parts.append(jnp.where(lane < LANES // 2, tile, -tile).astype(jnp.bfloat16))
    return jnp.concatenate(parts, 1)


def after_kernel(*refs):
    del refs


def after(first, *values):
    anywhere = pl.BlockSpec(memory_space=pl.ANY)
    return pl.pallas_call(
        after_kernel,
        in_specs=[anywhere] * (len(values) + len(first)),
        out_specs=[anywhere] * len(values),
        out_shape=[jax.ShapeDtypeStruct(v.shape, v.dtype) for v in values],
        input_output_aliases={i: i for i in range(len(values))},
        name="after",
    )(*values, *first)


def stack(scale, own, right):
    segments, rows = own.shape[0], own.shape[2]
    mine = jnp.concatenate([own[s, 0] for s in range(segments)], 1)
    left = jnp.concatenate([mine, rotated(mine)], 0)
    acc = lax.dot_general(left, right, (((1,), (1,)), ((), ())), preferred_element_type=jnp.float32)
    return (acc * scale).reshape(2, rows, acc.shape[1])


def cross_kernel(scale, hops, place, own, *refs):
    out, buf, sems = refs[-3:]
    step = pl.program_id(0)
    steps = pl.num_programs(0)
    slots = buf.shape[0]
    z, core = place[1], place[2]

    def copies(b):
        slot = lax.rem(b, slots)
        made = []
        if hops is None:
            for i in range(buf.shape[1]):
                made.append((refs[0].at[i, :, b], buf.at[slot, i]))
        else:
            for c in range(2):
                for i, (hop, start) in enumerate(hops):
                    piece = refs[len(hops) * c + i].at[:, b]
                    at = lax.rem(z + hop, 4) * 2 + (core if c == 0 else 1 - core)
                    made.append((piece, buf.at[slot, at, pl.ds(start, piece.shape[0])]))
        return [
            pltpu.make_async_copy(piece, to, sems.at[slot, i]) for i, (piece, to) in enumerate(made)
        ]

    @pl.when(step == 0)
    def _():
        for copy in copies(0):
            copy.start()

    for ahead in range(1, slots - 1):

        @pl.when((step == 0) & (ahead < steps))
        def _():
            for copy in copies(ahead):
                copy.start()

    @pl.when(step + slots - 1 < steps)
    def _():
        for copy in copies(step + slots - 1):
            copy.start()

    for copy in copies(step):
        copy.wait()

    slot = lax.rem(step, slots)
    segments = own.shape[0]
    columns = buf.shape[1] * buf.shape[3]
    right = [buf[slot, :, s].reshape(columns, LANES) for s in range(segments)]
    out[0] = stack(scale, own, jnp.concatenate(right, 1))


def cross(place, own, others, base, first_bin, hops=None, *, all_bins, chan, window_count):
    segments, bins, rows, lanes = own.shape
    half = chan // 2
    bases = [] if base is None else [base]
    anywhere = pl.BlockSpec(memory_space=pl.ANY)
    if not isinstance(others, list):
        others = [others]
    copies = half if hops is None else len(others)
    return pl.pallas_call(
        functools.partial(cross_kernel, 1.0 / window_count, hops),
        grid_spec=pltpu.PrefetchScalarGridSpec(
            num_scalar_prefetch=1,
            grid=(bins,),
            in_specs=[pl.BlockSpec((segments, 1, rows, lanes), lambda b, at: (0, b, 0, 0))]
            + [anywhere] * (len(others) + len(bases)),
            out_specs=pl.BlockSpec(
                (1, 2, rows, half * rows), lambda b, at: (b + first_bin, 0, 0, at[0])
            ),
            scratch_shapes=[
                pltpu.VMEM((SLOTS, half, segments, rows, lanes), own.dtype),
                pltpu.SemaphoreType.DMA((SLOTS, copies)),
            ],
        ),
        out_shape=jax.ShapeDtypeStruct((all_bins, 2, rows, chan * rows), jnp.float32),
        input_output_aliases={2 + len(others): 0} if bases else {},
        compiler_params=pltpu.CompilerParams(vmem_limit_bytes=56 * 1024 * 1024),
        cost_estimate=pl.CostEstimate(
            flops=4 * bins * rows * half * rows * segments * lanes,
            bytes_accessed=bins * half * rows * (2 * segments * lanes + 8 * rows),
            transcendentals=0,
        ),
        name="cross",
    )(place, own, *others, *bases)


def chan_index(x, z, c):
    return x * 8 + z * 2 + c


PLACES = [(x, z, c) for x in range(2) for z in range(4) for c in range(2)]
UP = [(chan_index(x, z, c), chan_index(x, (z + 1) % 4, c)) for x, z, c in PLACES]
DOWN = [(chan_index(x, z, c), chan_index(x, (z + 3) % 4, c)) for x, z, c in PLACES]
ACROSS = [(chan_index(x, z, c), chan_index(1 - x, z, c)) for x, z, c in PLACES]
SIBLING = [(chan_index(x, z, c), chan_index(x, z, 1 - c)) for x, z, c in PLACES]
X_HALVES = [list(range(8)), list(range(8, 16))]


def send(value, pairs):
    return lax.ppermute(value, "chan", pairs)


def gather(value):
    return lax.all_gather(value, "chan", axis_index_groups=X_HALVES)


def exchange(value):
    return lax.all_to_all(value, "seg", split_axis=0, concat_axis=0, tiled=True)


FIRST = 5
SPLIT = 4
SLOTS = 3


def local(strain_rate, window_starts):
    segments = lax.axis_size("seg")
    chan = lax.axis_size("chan")
    bins = F // segments
    spectra_b, spectra_a = local_spectra(strain_rate, window_starts, segments, FIRST)
    me = lax.axis_index("chan")
    z = lax.rem(me // 2, 4)
    core = lax.rem(me, 2)
    near = jnp.stack([me // 8, z, core])
    far = jnp.stack([1 - me // 8, z, core])

    count = segments * window_starts.shape[0]
    stacked = functools.partial(cross, all_bins=bins, chan=chan, window_count=count)

    half = segments // 2
    ring = [(0, 0), (3, 0), (1, 0), (2, 0), (2, half)]

    own_b = exchange(spectra_b)
    all_b = gather(own_b)
    far_b = [send(own_b, ACROSS)]
    (own_a,) = after([far_b[0]], exchange(spectra_a))
    own_a1, own_a2 = own_a[:, :SPLIT], own_a[:, SPLIT:]
    x_a = send(own_a, ACROSS)
    all_a1 = gather(own_a1)
    up_a2, down_a2 = send(own_a2, UP), send(own_a2, DOWN)
    hops = [
        lax.dynamic_index_in_dim(all_b, lax.rem(z + hop, 4) * 2 + core, 0, keepdims=False)
        for hop in range(1, 4)
    ]
    x_a, *hops = after([], x_a, *hops)
    all_xa = gather(x_a)
    far_b = far_b + [send(hop, ACROSS) for hop in hops]
    near_a2 = [own_a2, up_a2, down_a2, send(up_a2[:half], UP), send(down_a2[half:], DOWN)]
    near_a2 = near_a2 + [send(p, SIBLING) for p in near_a2]

    (near,) = after([far_b[1]], near)
    out = stacked(near, own_b, all_b, None, 0)
    out = stacked(near, own_a1, all_a1, out, FIRST)
    out = stacked(near, own_a2, near_a2, out, FIRST + SPLIT, ring)
    out, last = after([], out, far_b[3])
    far_b[3] = last
    far_b = far_b + [send(p, SIBLING) for p in far_b]
    out = stacked(far, own_b, far_b, out, 0, [(0, 0), (1, 0), (2, 0), (3, 0)])
    return stacked(far, own_a, all_xa, out, FIRST)


def solution(mesh):
    in_specs = (P("chan", "seg"), P("seg"))
    out_specs = P("seg", None, "chan", None)
    return jax.shard_map(local, mesh=mesh, in_specs=in_specs, out_specs=out_specs, check_vma=False)
```
